32 devices in a mesh: groups: 2 (over y), beam: 16 (over z, x, core).
Axes of the slice: x: 2, y: 2, z: 4, core: 2. Of those that a mesh axis runs over, the one named last changes fastest.
Arguments:
- potential: float32 [4, 512, 512], P('groups', 'beam'), parts along dimension 0, may hold values from -5 to 5
- beam_tilts: int32 [16, 2], replicated, may hold values from -16 to 16
- aperture: float32 [16], replicated, may hold values from 0.3 to 3
- aberration: float32 [16], replicated, may hold values from -3.140625 to 3.140625
- probe_spots: int32 [8, 32, 2], P('groups'), parts along dimension 0, may hold values from 0 to 127
- crop_anchor: int32 [4], P('groups'), parts along dimension 0, may hold values from 0 to 256
Outputs:
- diffraction: float32 [1024, 32, 128], P(('groups', 'beam')), parts along dimension 0
The draws below stay inside these ranges and needn't reach their ends.
There are 2 independent parts, one for each index of `groups`. The reference program is written for one: setup_inputs(seed, part) draws one part's arguments, and reference() takes and returns one part's arrays. A program takes and returns all parts, laid end to end along the dimension named above; an argument that names none is the same for every part. Nothing has to cross between parts.
Inputs may be any that keep to these rules, and one draw needn't show every extreme that they name: `probe_spots`: positions inside a tile. `crop_anchor`: the window lies inside the grid.
All inputs are finite; a program needn't handle non-finite values.
Results may differ from the reference program's by a relative error of at most 0.0003.
Values sent between devices are 32-bit elements; how exact they have to be, the bound alone decides.
A program may use at most 64 MiB of HBM per device.

```python
import math
import jax
import jax.numpy as jnp
from jax import lax

GRID = 512
CROP = 256
TILE = 128
LAYERS = 2
PROBES = 32
MAX_TILT = 16
TILES = 4
BEAMS = 16


def place_ends(array, rng, least, high):
    longest = array.shape.index(max(array.shape))
    spots = []
    for shift in (0, 1):
        where = [jax.random.randint(jax.random.fold_in(rng, axis), (), 0, length) for axis, length in enumerate(array.shape)]
        where[longest] = (where[longest] + shift) % array.shape[longest]
        spots.append(tuple(where))
    return array.at[spots[0]].set(least).at[spots[1]].set(high)


def levels(stream_key, shape, split, low, top_value):
    def one(axis_at, blocks):
        draws = jax.random.uniform(jax.random.fold_in(jax.random.fold_in(stream_key, 6), axis_at), (blocks,), jnp.float32, low / len(split), top_value / len(split))
        return jnp.repeat(jnp.exp(draws), shape[axis_at] // blocks).reshape((-1,) + (1,) * (len(shape) - axis_at - 1))

    loudness = one(*split[0])
    for cut in split[1:]:
        loudness = loudness * one(*cut)
    return loudness


def gaussian(stream_key, dims, width, reach, shards=(), held_as=jnp.bfloat16):
    drawn = jax.random.normal(stream_key, dims, jnp.float32) * width
    if len(shards) > 0:
        drawn = levels(stream_key, dims, shards, -0.22, 0.18) * drawn
    return jnp.clip(drawn, min=-reach, max=reach).astype(held_as)


def setup_inputs(seed: int = 0, part: int = 0) -> dict:
    seeds = jax.random.split(jax.random.key(seed), 7)
    part_keys = jax.random.split(jax.random.fold_in(seeds[6], part), 7)
    return {
        "potential": gaussian(part_keys[0], (LAYERS, GRID, GRID), 1.0, 5.0, ((1, 16),), jnp.float32),
        "beam_tilts": place_ends(jax.random.randint(seeds[1], (BEAMS, 2), 0 - MAX_TILT, MAX_TILT + 1), jax.random.fold_in(seeds[1], 1), 0 - MAX_TILT, MAX_TILT).astype(jnp.int32),
        "aperture": jnp.clip(jnp.exp(jax.random.uniform(seeds[2], (BEAMS,), jnp.float32, math.log(0.3), math.log(3.0))), 0.3, 3.0),
        "aberration": jnp.clip(jax.random.uniform(seeds[3], (BEAMS,), jnp.float32, -3.140625, 3.140625), -3.140625, 3.140625),
        "probe_spots": place_ends(jax.random.randint(part_keys[4], (TILES, PROBES, 2), 0, TILE), jax.random.fold_in(part_keys[4], 1), 0, TILE - 1).astype(jnp.int32),
        "crop_anchor": jax.random.randint(part_keys[5], (2,), 0, GRID - CROP + 1).astype(jnp.int32),
    }


def reference(potential, beam_tilts, aperture, aberration, probe_spots, crop_anchor):
    coords = jnp.arange(GRID, dtype=jnp.int32)
    frequency = jnp.where(coords < GRID // 2, coords, coords - GRID)
    square = frequency[:, None] ** 2 + frequency[None, :] ** 2
    phase_angle = (jnp.pi / GRID) * jnp.remainder(square, 2 * GRID).astype(jnp.float32)
    passing = 9 * square < GRID * GRID
    propagator = jnp.where(passing, jnp.cos(phase_angle) - 1j * jnp.sin(phase_angle), 0.0)
    transmit = jnp.cos(potential) + 1j * jnp.sin(potential)
    per_side = CROP // TILE

    def one_beam(tilt_pair):
        plane_phase = jnp.remainder(tilt_pair[0] * coords[:, None] + tilt_pair[1] * coords[None, :], GRID)
        plane_angle = (2.0 * jnp.pi / GRID) * plane_phase.astype(jnp.float32)
        wave_field = jnp.cos(plane_angle) + 1j * jnp.sin(plane_angle)
        for layer_index in range(LAYERS):
            wave_field = wave_field * transmit[layer_index]
            if layer_index + 1 < LAYERS:
                wave_field = jnp.fft.ifft2(propagator * jnp.fft.fft2(wave_field))
        cropped = lax.dynamic_slice(wave_field, (crop_anchor[0], crop_anchor[1]), (CROP, CROP))
        tile_stack = cropped.reshape(per_side, TILE, per_side, TILE).transpose(0, 2, 1, 3).reshape(TILES, TILE, TILE)
        return jnp.real(tile_stack), jnp.imag(tile_stack)

    beam_real, beam_imag = lax.map(one_beam, beam_tilts)
    tile_ids = jnp.arange(TILES, dtype=jnp.int32)
    anchor_rows = crop_anchor[0] + TILE * (tile_ids // per_side)
    anchor_cols = crop_anchor[1] + TILE * (tile_ids % per_side)
    spot_rows = anchor_rows[:, None] + probe_spots[:, :, 0]
    spot_cols = anchor_cols[:, None] + probe_spots[:, :, 1]
    phase_index = jnp.remainder(spot_rows[:, :, None] * beam_tilts[None, None, :, 0] + spot_cols[:, :, None] * beam_tilts[None, None, :, 1], GRID)
    weight_angle = aberration[None, None, :] - (2.0 * jnp.pi / GRID) * phase_index.astype(jnp.float32)
    weight_real = aperture[None, None, :] * jnp.cos(weight_angle)
    weight_imag = aperture[None, None, :] * jnp.sin(weight_angle)
    precise = lax.Precision.HIGHEST
    exit_real = jnp.einsum("tpb,btyx->tpyx", weight_real, beam_real, precision=precise) - jnp.einsum("tpb,btyx->tpyx", weight_imag, beam_imag, precision=precise)
    exit_imag = jnp.einsum("tpb,btyx->tpyx", weight_real, beam_imag, precision=precise) + jnp.einsum("tpb,btyx->tpyx", weight_imag, beam_real, precision=precise)
    spectrum = jnp.fft.fft2(exit_real + 1j * exit_imag)
    intensity = jnp.real(spectrum) ** 2 + jnp.imag(spectrum) ** 2
    level = jnp.mean(intensity, axis=(2, 3), keepdims=True)
    normed = intensity / (level + 1e-6)
    return normed.transpose(0, 2, 1, 3).reshape(TILES * TILE, PROBES, TILE)
```

```python
import functools

import jax
import jax.numpy as jnp
import numpy as np
from jax import lax
from jax.experimental import pallas as pl
from jax.experimental.pallas import tpu as pltpu
from jax.sharding import PartitionSpec as P

CROP = 256
TILE = 128
MAX_TILT = 16
F32 = jnp.float32
BF16 = jnp.bfloat16
MESH = pl.DeviceIdType.MESH
LIMIT = 56 * 1024 * 1024


def split(value):
    high = value.astype(BF16)
    return high, (value - high.astype(F32)).astype(BF16)


def np_split(value):
    value = value.astype(np.float32)
    high = value.astype(BF16)
    return high, (value - high.astype(np.float32)).astype(BF16)


def mm(left, right):
    return jnp.dot(left, right, preferred_element_type=F32)


def polys(r):
    s = r * r
    sin = r + r * s * (-1.0 / 6 + s * (1.0 / 120 + s * (-1.0 / 5040 + s * (1.0 / 362880))))
    cos = 1.0 + s * (-0.5 + s * (1.0 / 24 + s * (-1.0 / 720 + s * (1.0 / 40320))))
    return cos, sin


def cos_sin(x):
    q = jnp.floor(x * (2.0 / np.pi) + 0.5)
    r = (x - q * 1.5703125) - q * 4.838267948966e-4
    cos, sin = polys(r)
    half = q * 0.5
    whole = jnp.floor(half)
    odd = half != whole
    c = jnp.where(odd, sin, cos)
    s = jnp.where(odd, cos, sin)
    quarter = jnp.floor(half * 0.5)
    upper = (whole - 2.0 * quarter) > 0.5
    flip_c = odd != upper
    return jnp.where(flip_c, -c, c), jnp.where(upper, -s, s)


def cos_sin_int(m, period):
    m = m & (period - 1)
    quarter = period // 4
    q = lax.shift_right_logical(
        m + quarter // 2, int(np.log2(quarter))
    )
    r = (m - q * quarter).astype(F32) * (2.0 * np.pi / period)
    cos, sin = polys(r)
    odd = (q & 1) == 1
    c = jnp.where(odd, sin, cos)
    s = jnp.where(odd, cos, sin)
    return jnp.where(((q + 1) & 2) == 2, -c, c), jnp.where((q & 2) == 2, -s, s)


def half_band(length):
    reach = int(np.sqrt((length * length - 1) // 9)) + MAX_TILT
    return -(-(reach + 1) // 64) * 64


def forward_tables(length):
    half = half_band(length)
    grid = np.arange(length)
    k = np.arange(-half, half)
    angle = 2 * np.pi / length * ((grid[:, None] * k[None, :]) % length)
    c, s = np.cos(angle), np.sin(angle)
    cols = np.concatenate(
        (np.concatenate((c, -s), 1), np.concatenate((s, c), 1)), 0
    )
    k = np.arange(half)
    angle = 2 * np.pi / length * ((k[:, None] * grid[None, :]) % length)
    rows = np.concatenate((np.cos(angle), np.sin(angle)), 0)
    return np_split(cols) + np_split(rows)


def forward_kernel(
    n, remote, own_ref, crop_ref, ch_any, cl_any, rh_any, rl_any, qh_ref, ql_ref, *rest
):
    if remote:
        t1_ref, buf, buf1, ch, cl, rh, rl, th, tl, uh, ul, tab_sem, s0, r0, s1, r1 = rest
    else:
        ch, cl, rh, rl, th, tl, uh, ul, tab_sem = rest
    pairs = ((ch_any, ch), (cl_any, cl), (rh_any, rh), (rl_any, rl))
    tables = [
        pltpu.make_async_copy(src, dst, tab_sem.at[i]) for i, (src, dst) in enumerate(pairs)
    ]
    for copy in tables:
        copy.start()
    length = th.shape[0]
    half = rh.shape[0] // 2
    band = 2 * half

    def transmit(value, row, count):
        c, s = cos_sin(value)
        h, l = split(c)
        th[pl.ds(row, count), :length] = h
        tl[pl.ds(row, count), :length] = l
        h, l = split(s)
        th[pl.ds(row, count), length:] = h
        tl[pl.ds(row, count), length:] = l

    if remote:
        rows = own_ref.shape[0]
        groups = lax.axis_index("groups")
        me = lax.axis_index("beam")
        planes = n // 4
        plane, low = me // 4, me % 4
        across = plane * 4 + (low + 2) % 4
        sibling = plane * 4 + (low // 2) * 2 + (1 - low % 2)

        def peer(step):
            return ((plane + step) % planes) * 4 + low

        barrier = pltpu.get_barrier_semaphore()
        friends = [across, sibling] + [peer(step) for step in range(1, planes)]
        for friend in friends:
            pl.semaphore_signal(barrier, inc=1, device_id=(groups, friend), device_id_type=MESH)
        pl.semaphore_wait(barrier, len(friends))

        def push(which, src, block, target, send_index):
            dst, ss, rs = ((buf, s0, r0), (buf1, s1, r1))[which]
            return pltpu.make_async_remote_copy(
                src_ref=src,
                dst_ref=dst.at[block],
                send_sem=ss.at[send_index],
                recv_sem=rs.at[block],
                device_id=(groups, target),
                device_id_type=MESH,
            )

        started = []

        def go(which, src, block, target, index):
            copy = push(which, src, block, target, index)
            copy.start()
            started.append(copy)

        def arrive(which, block):
            src = (own_ref, crop_ref)[which]
            push(which, src, block, sibling, 0).wait_recv()

        order = [1, planes - 1] + [s for s in range(2, planes - 1)]
        order = [s for i, s in enumerate(order) if s not in order[:i]]

        def open_round(which):
            src = (own_ref, crop_ref)[which]
            go(which, src, me, across, 0)
            for i, step in enumerate(order):
                go(which, src, me, peer(step), 1 + i)
            go(which, src, me, sibling, planes)

        def forward_round(which, work):
            dst = (buf, buf1)[which]
            index = planes + 1
            work(me, (own_ref, crop_ref)[which])
            for step in [0] + order:
                base = ((plane + step) % planes) * 4
                if step != 0:
                    block = base + low
                    arrive(which, block)
                    go(which, dst.at[block], block, across, index)
                    go(which, dst.at[block], block, sibling, index + 1)
                    index += 2
                    work(block, dst.at[block])
                block = base + (low + 2) % 4
                arrive(which, block)
                go(which, dst.at[block], block, sibling, index)
                index += 1
                work(block, dst.at[block])
            for step in [0] + order:
                base = ((plane + step) % planes) * 4
                for block in (
                    base + (low // 2) * 2 + (1 - low % 2),
                    base + (1 - low // 2) * 2 + (1 - low % 2),
                ):
                    arrive(which, block)
                    work(block, dst.at[block])

        def work0(block, ref):
            transmit(ref[...], pl.multiple_of(block * rows, rows), rows)

        def work1(block, ref):
            t1_ref[pl.ds(pl.multiple_of(block * rows, rows), rows), :] = ref[...]

        open_round(0)
        forward_round(0, work0)
        open_round(1)
    else:
        transmit(own_ref[...], 0, length)

    for copy in tables:
        copy.wait()

    step_rows = 256

    def stage_one(i, carry):
        at = pl.multiple_of(i * step_rows, step_rows)
        h = th[pl.ds(at, step_rows), :]
        l = tl[pl.ds(at, step_rows), :]
        u = mm(h, ch[...]) + mm(l, ch[...]) + mm(h, cl[...])
        high, lower = split(u)
        uh[pl.ds(at, step_rows), :] = high
        ul[pl.ds(at, step_rows), :] = lower
        return carry

    lax.fori_loop(0, length // step_rows, stage_one, 0)
    if remote:
        forward_round(1, work1)
    for j in range(band // 128):
        a, b = slice(j * 128, j * 128 + 128), slice(band + j * 128, band + j * 128 + 128)
        h = jnp.concatenate((uh[:, a], uh[:, b]), 1)
        l = jnp.concatenate((ul[:, a], ul[:, b]), 1)
        p = mm(rh[...], h) + mm(rh[...], l) + mm(rl[...], h)
        cr, ci, sr, si = p[:half, :128], p[:half, 128:], p[half:, :128], p[half:, 128:]
        for at, real, imag in ((0, cr + si, ci - sr), (half, cr - si, ci + sr)):
            h, l = split(real)
            qh_ref[at : at + half, a] = h
            ql_ref[at : at + half, a] = l
            h, l = split(imag)
            qh_ref[at : at + half, b] = h
            ql_ref[at : at + half, b] = l
    if remote:
        for copy in started:
            copy.wait_send()


def forward(own, crop, n, length):
    rows = own.shape[0]
    half = half_band(length)
    band = 2 * half
    remote = rows % 16 == 0 and n % 4 == 0 and n > 4
    tables = [jnp.asarray(t) for t in forward_tables(length)]
    vmem = pl.BlockSpec(memory_space=pltpu.VMEM)
    scratch = [
        pltpu.VMEM((2 * length, 2 * band), BF16),
        pltpu.VMEM((2 * length, 2 * band), BF16),
        pltpu.VMEM((band, length), BF16),
        pltpu.VMEM((band, length), BF16),
        pltpu.VMEM((length, 2 * length), BF16),
        pltpu.VMEM((length, 2 * length), BF16),
        pltpu.VMEM((length, 2 * band), BF16),
        pltpu.VMEM((length, 2 * band), BF16),
        pltpu.SemaphoreType.DMA((4,)),
    ]
    outs = [jax.ShapeDtypeStruct((band, 2 * band), BF16)] * 2
    if remote:
        outs = outs + [jax.ShapeDtypeStruct((length, CROP), F32)]
        scratch = (
            [pltpu.VMEM((n, rows, length), F32), pltpu.VMEM((n, rows, CROP), F32)]
            + scratch
            + [pltpu.SemaphoreType.DMA((n,))] * 4
        )
        params = pltpu.CompilerParams(
            collective_id=0, has_side_effects=True, vmem_limit_bytes=LIMIT
        )
    else:
        own = lax.all_gather(own, "beam", axis=0, tiled=True)
        params = pltpu.CompilerParams(vmem_limit_bytes=LIMIT)
    result = pl.pallas_call(
        functools.partial(forward_kernel, n, remote),
        out_shape=outs,
        in_specs=[vmem, vmem] + [pl.BlockSpec(memory_space=pl.ANY)] * 4,
        out_specs=[vmem] * len(outs),
        scratch_shapes=scratch,
        compiler_params=params,
        name="forward",
    )(own, crop, *tables)
    if remote:
        return result
    return (*result, lax.all_gather(crop, "beam", axis=0, tiled=True))


def tile_tables():
    k = np.arange(TILE)
    angle = 2 * np.pi / TILE * ((k[:, None] * k[None, :]) % TILE)
    c, s = np.cos(angle), np.sin(angle)
    cols = np.concatenate((np.concatenate((c, -s), 1), np.concatenate((s, c), 1)), 0)
    rh, rl = np_split(np.concatenate((c, -s), 0))
    return np_split(cols) + (np.concatenate((rh, rh, rl), 1),)


def beam_kernel(
    length, beams, info, tilts, qh_ref, ql_ref, t1_ref, dh, dl, drow, spots, weights,
    out_ref, tr, ti, gcat, sr, si,
):
    beam = pl.program_id(0)
    band = qh_ref.shape[0]
    half = band // 2
    row0, col0, ky0 = info[0], info[1], info[2]
    ty, tx = tilts[2 * beam], tilts[2 * beam + 1]
    period = 2 * length

    @pl.when(beam == 0)
    def _():
        c, s = cos_sin(t1_ref[...])
        tr[...] = c
        ti[...] = s

    f = lax.broadcasted_iota(jnp.int32, (band, TILE), 0) - half + tx
    cell = lax.broadcasted_iota(jnp.int32, (band, TILE), 1) + col0
    c, s = cos_sin_int(f * (2 * cell - f), period)
    chi, clo = split(c)
    shi, slo = split(s)
    xh = jnp.concatenate(
        (jnp.concatenate((chi, shi), 1), jnp.concatenate((-shi, chi), 1)), 0
    )
    xl = jnp.concatenate(
        (jnp.concatenate((clo, slo), 1), jnp.concatenate((-slo, clo), 1)), 0
    )
    k = lax.broadcasted_iota(jnp.int32, (TILE, band), 1)
    f = jnp.where(k < half, k, half - k) + ty
    cell = lax.broadcasted_iota(jnp.int32, (TILE, band), 0) + row0
    c, s = cos_sin_int(f * (2 * cell - f), period)
    c = jnp.where(k == half, 0.0, c)
    s = jnp.where(k == half, 0.0, s)
    chi, clo = split(c)
    shi, slo = split(s)
    yh = jnp.concatenate((chi, shi), 0)
    yl = jnp.concatenate((clo, slo), 0)

    fx = (lax.broadcasted_iota(jnp.int32, (1, band), 1) - half + tx).astype(F32)
    fx2 = 9.0 * fx * fx
    chunk = 128
    for i in range(band // chunk):
        at = slice(i * chunk, i * chunk + chunk)
        k = lax.broadcasted_iota(jnp.int32, (chunk, 1), 0) + i * chunk
        fy = (jnp.where(k < half, k, half - k) + ty).astype(F32)
        keep = jnp.where(9.0 * fy * fy + fx2 < float(length * length), 1.0, 0.0).astype(BF16)
        keep = jnp.concatenate((keep, keep), 1)
        h = qh_ref[at, :] * keep
        l = ql_ref[at, :] * keep
        g = mm(h, xh) + mm(l, xh) + mm(h, xl)
        gh, gl = split(g)
        gcat[i * chunk : i * chunk + chunk, :] = gh
        gcat[band + i * chunk : band + i * chunk + chunk, :] = gl
        gcat[2 * band + i * chunk : 2 * band + i * chunk + chunk, :] = gh
    p = mm(jnp.concatenate((yh, yh, yl), 1), gcat[...])
    wr = p[:TILE, :TILE] - p[TILE:, TILE:]
    wi = p[:TILE, TILE:] + p[TILE:, :TILE]
    a, b = tr[...], ti[...]
    w = jnp.concatenate((wr * a - wi * b, wr * b + wi * a), 1)
    h, l = split(w)
    v = mm(h, dh[...]) + mm(l, dh[...]) + mm(h, dl[...])
    h, l = split(v)
    z = mm(drow[...], jnp.concatenate((h, l, h), 0))
    sr[pl.ds(beam, TILE, stride=beams), :] = z[:TILE, :TILE] - z[TILE:, TILE:]
    si[pl.ds(beam, TILE, stride=beams), :] = z[:TILE, TILE:] + z[TILE:, :TILE]

    @pl.when(beam == beams - 1)
    def _():
        probes = spots.shape[0]
        q = (spots[:, 0:1] + row0) * 1
        r = (spots[:, 1:2] + col0) * 1
        phase = weights[0:1, :].astype(jnp.int32) * q + weights[1:2, :].astype(jnp.int32) * r
        phase = (phase & (length - 1)).astype(F32)
        c, s = cos_sin(weights[3:4, :] - phase * (2.0 * np.pi / length))
        amp = weights[2:3, :] * (1.0 / (length * length))
        full = jnp.concatenate((c * amp, s * amp), 0)
        h = full.astype(BF16).astype(F32)
        lane = lax.broadcasted_iota(jnp.int32, full.shape, 1)
        coef = jnp.where(lane < 2 * beams, h, full - h).astype(BF16)

        def one(ky):
            at = pl.multiple_of(ky * beams, beams)
            both = jnp.concatenate((sr[pl.ds(at, beams), :], si[pl.ds(at, beams), :]), 1)
            h, l = split(both)
            e = mm(coef, jnp.concatenate((h, l, h), 0))
            er = e[:probes, :TILE] - e[probes:, TILE:]
            ei = e[:probes, TILE:] + e[probes:, :TILE]
            return er * er + ei * ei

        own = out_ref.shape[0]

        def mine(j, total):
            value = one(ky0 + j)
            out_ref[j] = value
            return total + value

        def others(j, total):
            return total + one((ky0 + own + j) & (TILE - 1))

        total = lax.fori_loop(0, own, mine, jnp.zeros((probes, TILE), F32), unroll=4)
        total = lax.fori_loop(0, TILE - own, others, total, unroll=4)
        level = jnp.sum(total, axis=1, keepdims=True) * (1.0 / (TILE * TILE))
        scale = 1.0 / (level + 1e-06)

        def norm(j, carry):
            out_ref[j] = out_ref[j] * scale
            return carry

        lax.fori_loop(0, own, norm, 0, unroll=4)


def per_device(potential, beam_tilts, aperture, aberration, probe_spots, crop_anchor, n):
    length = potential.shape[2]
    beams = beam_tilts.shape[0]
    per_side = CROP // TILE
    device = lax.axis_index("beam")
    crop_rows = lax.dynamic_slice(potential[1], (0, crop_anchor[1]), (potential.shape[1], CROP))
    qh, ql, t1 = forward(potential[0], crop_rows, n, length)
    own = per_side * per_side * TILE // n
    my_tile = device * own // TILE
    row0 = crop_anchor[0] + TILE * (my_tile // per_side)
    col_at = TILE * (my_tile % per_side)
    col0 = crop_anchor[1] + col_at
    t1 = lax.dynamic_slice(t1, (row0, col_at), (TILE, TILE))
    spots = lax.dynamic_slice_in_dim(probe_spots, my_tile, 1, 0)[0]
    info = jnp.stack((row0, col0, device * own % TILE))
    weights = jnp.concatenate(
        (beam_tilts.T.astype(F32), aperture[None], aberration[None]), 0
    )
    weights = jnp.concatenate((weights,) * 3, 1)
    dh, dl, drow = [jnp.asarray(t) for t in tile_tables()]
    probes = spots.shape[0]
    smem = pl.BlockSpec(memory_space=pltpu.SMEM)
    vmem = pl.BlockSpec(memory_space=pltpu.VMEM)
    return pl.pallas_call(
        functools.partial(beam_kernel, length, beams),
        grid=(beams,),
        out_shape=jax.ShapeDtypeStruct((own, probes, TILE), F32),
        in_specs=[smem, smem] + [vmem] * 8,
        out_specs=vmem,
        scratch_shapes=[
            pltpu.VMEM((TILE, TILE), F32),
            pltpu.VMEM((TILE, TILE), F32),
            pltpu.VMEM((3 * qh.shape[0], 2 * TILE), BF16),
            pltpu.VMEM((TILE * beams, TILE), F32),
            pltpu.VMEM((TILE * beams, TILE), F32),
        ],
        compiler_params=pltpu.CompilerParams(vmem_limit_bytes=LIMIT),
        name="beams",
    )(info, beam_tilts.reshape(-1), qh, ql, t1, dh, dl, drow, spots, weights)


def solution(mesh):
    placed = (P("groups", "beam", None), P(), P(), P(), P("groups", None, None), P("groups"))
    return jax.shard_map(
        functools.partial(per_device, n=mesh.shape["beam"]),
        mesh=mesh,
        in_specs=placed,
        out_specs=P(("groups", "beam"), None, None),
        check_vma=False,
    )
```

```python
import functools

import jax
import jax.numpy as jnp
import numpy as np
from jax import lax
from jax.experimental import pallas as pl
from jax.experimental.pallas import tpu as pltpu
from jax.sharding import PartitionSpec as P

CROP = 256
TILE = 128
MAX_TILT = 16
F32 = jnp.float32
BF16 = jnp.bfloat16
MESH = pl.DeviceIdType.MESH
LIMIT = 56 * 1024 * 1024


def split(value):
    high = value.astype(BF16)
    return high, (value - high.astype(F32)).astype(BF16)


def np_split(value):
    value = value.astype(np.float32)
    high = value.astype(BF16)
    return high, (value - high.astype(np.float32)).astype(BF16)


def mm(left, right):
    return jnp.dot(left, right, preferred_element_type=F32)


def polys(r):
    s = r * r
    sin = r + r * s * (-1.0 / 6 + s * (1.0 / 120 + s * (-1.0 / 5040 + s * (1.0 / 362880))))
    cos = 1.0 + s * (-0.5 + s * (1.0 / 24 + s * (-1.0 / 720 + s * (1.0 / 40320))))
    return cos, sin


def cos_sin(x):
    q = jnp.floor(x * (2.0 / np.pi) + 0.5)
    r = (x - q * 1.5703125) - q * 4.838267948966e-4
    cos, sin = polys(r)
    half = q * 0.5
    whole = jnp.floor(half)
    odd = half != whole
    c = jnp.where(odd, sin, cos)
    s = jnp.where(odd, cos, sin)
    quarter = jnp.floor(half * 0.5)
    upper = (whole - 2.0 * quarter) > 0.5
    flip_c = odd != upper
    return jnp.where(flip_c, -c, c), jnp.where(upper, -s, s)


def cos_sin_int(m, period):
    m = m & (period - 1)
    quarter = period // 4
    q = lax.shift_right_logical(
        m + quarter // 2, int(np.log2(quarter))
    )
    r = (m - q * quarter).astype(F32) * (2.0 * np.pi / period)
    cos, sin = polys(r)
    odd = (q & 1) == 1
    c = jnp.where(odd, sin, cos)
    s = jnp.where(odd, cos, sin)
    return jnp.where(((q + 1) & 2) == 2, -c, c), jnp.where((q & 2) == 2, -s, s)


def half_band(length):
    reach = int(np.sqrt((length * length - 1) // 9)) + MAX_TILT
    return -(-(reach + 1) // 64) * 64


def forward_tables(length):
    half = half_band(length)
    grid = np.arange(length)
    k = np.arange(-half, half)
    angle = 2 * np.pi / length * ((grid[:, None] * k[None, :]) % length)
    c, s = np.cos(angle), np.sin(angle)
    cols = np.concatenate(
        (np.concatenate((c, -s), 1), np.concatenate((s, c), 1)), 0
    )
    k = np.arange(half)
    angle = 2 * np.pi / length * ((k[:, None] * grid[None, :]) % length)
    rows = np.concatenate((np.cos(angle), np.sin(angle)), 0)
    return np_split(cols) + np_split(rows)


def forward_kernel(
    n, remote, own_ref, crop_ref, ch_any, cl_any, rh_any, rl_any, qh_ref, ql_ref, *rest
):
    if remote:
        t1_ref, buf, buf1, ch, cl, rh, rl, th, tl, uh, ul, tab_sem, s0, r0, s1, r1 = rest
    else:
        ch, cl, rh, rl, th, tl, uh, ul, tab_sem = rest
    pairs = ((ch_any, ch), (cl_any, cl), (rh_any, rh), (rl_any, rl))
    tables = [
        pltpu.make_async_copy(src, dst, tab_sem.at[i]) for i, (src, dst) in enumerate(pairs)
    ]
    for copy in tables:
        copy.start()
    length = th.shape[0]
    half = rh.shape[0] // 2
    band = 2 * half

    def transmit(value, row, count):
        c, s = cos_sin(value)
        h, l = split(c)
        th[pl.ds(row, count), :length] = h
        tl[pl.ds(row, count), :length] = l
        h, l = split(s)
        th[pl.ds(row, count), length:] = h
        tl[pl.ds(row, count), length:] = l

    if remote:
        rows = own_ref.shape[0]
        groups = lax.axis_index("groups")
        me = lax.axis_index("beam")
        planes = n // 4
        plane, low = me // 4, me % 4
        across = plane * 4 + (low + 2) % 4
        sibling = plane * 4 + (low // 2) * 2 + (1 - low % 2)

        def peer(step):
            return ((plane + step) % planes) * 4 + low

        barrier = pltpu.get_barrier_semaphore()
        friends = [across, sibling] + [peer(step) for step in range(1, planes)]
        for friend in friends:
            pl.semaphore_signal(barrier, inc=1, device_id=(groups, friend), device_id_type=MESH)
        pl.semaphore_wait(barrier, len(friends))

        def push(which, src, block, target, send_index):
            dst, ss, rs = ((buf, s0, r0), (buf1, s1, r1))[which]
            return pltpu.make_async_remote_copy(
                src_ref=src,
                dst_ref=dst.at[block],
                send_sem=ss.at[send_index],
                recv_sem=rs.at[block],
                device_id=(groups, target),
                device_id_type=MESH,
            )

        def own_part(which, target):
            return own_ref if which == 0 else crop_ref.at[(target // 4) % (CROP // TILE)]

        started = []

        def go(which, src, block, target, index):
            copy = push(which, src, block, target, index)
            copy.start()
            started.append(copy)

        def arrive(which, block):
            push(which, own_part(which, me), block, sibling, 0).wait_recv()

        order = [1, planes - 1] + [s for s in range(2, planes - 1)]
        order = [s for i, s in enumerate(order) if s not in order[:i]]

        def open_round(which):
            go(which, own_part(which, me), me, across, 0)
            for i, step in enumerate(order):
                go(which, own_part(which, peer(step)), me, peer(step), 1 + i)
            go(which, own_part(which, me), me, sibling, planes)

        def forward_round(which, work):
            dst = (buf, buf1)[which]
            index = planes + 1
            work(me, own_part(which, me))
            for step in [0] + order:
                base = ((plane + step) % planes) * 4
                if step != 0:
                    block = base + low
                    arrive(which, block)
                    go(which, dst.at[block], block, across, index)
                    go(which, dst.at[block], block, sibling, index + 1)
                    index += 2
                    work(block, dst.at[block])
                block = base + (low + 2) % 4
                arrive(which, block)
                go(which, dst.at[block], block, sibling, index)
                index += 1
                work(block, dst.at[block])
            for step in [0] + order:
                base = ((plane + step) % planes) * 4
                for block in (
                    base + (low // 2) * 2 + (1 - low % 2),
                    base + (1 - low // 2) * 2 + (1 - low % 2),
                ):
                    arrive(which, block)
                    work(block, dst.at[block])

        def work0(block, ref):
            transmit(ref[...], pl.multiple_of(block * rows, rows), rows)

        def work1(block, ref):
            t1_ref[pl.ds(pl.multiple_of(block * rows, rows), rows), :] = ref[...]

        open_round(0)
        open_round(1)
        forward_round(0, work0)
    else:
        transmit(own_ref[...], 0, length)

    for copy in tables:
        copy.wait()

    step_rows = 256

    def stage_one(i, carry):
        at = pl.multiple_of(i * step_rows, step_rows)
        h = th[pl.ds(at, step_rows), :]
        l = tl[pl.ds(at, step_rows), :]
        u = mm(h, ch[...]) + mm(l, ch[...]) + mm(h, cl[...])
        high, lower = split(u)
        uh[pl.ds(at, step_rows), :] = high
        ul[pl.ds(at, step_rows), :] = lower
        return carry

    lax.fori_loop(0, length // step_rows, stage_one, 0)
    if remote:
        forward_round(1, work1)
    for j in range(band // 128):
        a, b = slice(j * 128, j * 128 + 128), slice(band + j * 128, band + j * 128 + 128)
        h = jnp.concatenate((uh[:, a], uh[:, b]), 1)
        l = jnp.concatenate((ul[:, a], ul[:, b]), 1)
        p = mm(rh[...], h) + mm(rh[...], l) + mm(rl[...], h)
        cr, ci, sr, si = p[:half, :128], p[:half, 128:], p[half:, :128], p[half:, 128:]
        for at, real, imag in ((0, cr + si, ci - sr), (half, cr - si, ci + sr)):
            h, l = split(real)
            qh_ref[at : at + half, a] = h
            ql_ref[at : at + half, a] = l
            h, l = split(imag)
            qh_ref[at : at + half, b] = h
            ql_ref[at : at + half, b] = l
    if remote:
        for copy in started:
            copy.wait_send()


def forward(own, crop, n, length):
    rows = own.shape[0]
    half = half_band(length)
    band = 2 * half
    remote = rows % 16 == 0 and n == 4 * (CROP // TILE) ** 2
    tables = [jnp.asarray(t) for t in forward_tables(length)]
    vmem = pl.BlockSpec(memory_space=pltpu.VMEM)
    scratch = [
        pltpu.VMEM((2 * length, 2 * band), BF16),
        pltpu.VMEM((2 * length, 2 * band), BF16),
        pltpu.VMEM((band, length), BF16),
        pltpu.VMEM((band, length), BF16),
        pltpu.VMEM((length, 2 * length), BF16),
        pltpu.VMEM((length, 2 * length), BF16),
        pltpu.VMEM((length, 2 * band), BF16),
        pltpu.VMEM((length, 2 * band), BF16),
        pltpu.SemaphoreType.DMA((4,)),
    ]
    outs = [jax.ShapeDtypeStruct((band, 2 * band), BF16)] * 2
    if remote:
        outs = outs + [jax.ShapeDtypeStruct((length, TILE), F32)]
        scratch = (
            [pltpu.VMEM((n, rows, length), F32), pltpu.VMEM((n, rows, TILE), F32)]
            + scratch
            + [pltpu.SemaphoreType.DMA((n,))] * 4
        )
        params = pltpu.CompilerParams(
            collective_id=0, has_side_effects=True, vmem_limit_bytes=LIMIT
        )
    else:
        own = lax.all_gather(own, "beam", axis=0, tiled=True)
        params = pltpu.CompilerParams(vmem_limit_bytes=LIMIT)
    result = pl.pallas_call(
        functools.partial(forward_kernel, n, remote),
        out_shape=outs,
        in_specs=[vmem, vmem] + [pl.BlockSpec(memory_space=pl.ANY)] * 4,
        out_specs=[vmem] * len(outs),
        scratch_shapes=scratch,
        compiler_params=params,
        name="forward",
    )(own, crop, *tables)
    if remote:
        return result
    tile = lax.axis_index("beam") * (CROP // TILE) ** 2 // n
    crop = lax.dynamic_index_in_dim(
        lax.all_gather(crop, "beam", axis=1, tiled=True), tile % (CROP // TILE), 0, False
    )
    return (*result, crop)


def tile_tables():
    k = np.arange(TILE)
    angle = 2 * np.pi / TILE * ((k[:, None] * k[None, :]) % TILE)
    c, s = np.cos(angle), np.sin(angle)
    cols = np.concatenate((np.concatenate((c, -s), 1), np.concatenate((s, c), 1)), 0)
    rh, rl = np_split(np.concatenate((c, -s), 0))
    return np_split(cols) + (np.concatenate((rh, rh, rl), 1),)


def beam_kernel(
    length, beams, n, tilts, anchor, qh_ref, ql_ref, t1_ref, dh, dl, drow, spots_ref, weights,
    out_ref, tr, ti, gcat, sr, si, sent, got, send_sem, recv_sem,
):
    step = pl.program_id(0)
    steps = beams // 2
    groups = lax.axis_index("groups")
    me = lax.axis_index("beam")
    core = me % 2
    sibling = me + 1 - 2 * core
    beam = core * steps + step
    own = out_ref.shape[0]
    per_side = CROP // TILE
    my_tile = me * own // TILE
    ky0 = me * own % TILE
    col_at = pl.multiple_of((my_tile % per_side) * TILE, TILE)
    row0 = anchor[0] + TILE * (my_tile // per_side)
    col0 = anchor[1] + col_at
    band = qh_ref.shape[0]
    half = band // 2
    ty, tx = tilts[beam, 0], tilts[beam, 1]
    period = 2 * length

    def share(at):
        return pltpu.make_async_remote_copy(
            src_ref=sent.at[at],
            dst_ref=got.at[at],
            send_sem=send_sem.at[at],
            recv_sem=recv_sem.at[at],
            device_id=(groups, sibling),
            device_id_type=MESH,
        )

    @pl.when(step == 0)
    def _():
        barrier = pltpu.get_barrier_semaphore()
        pl.semaphore_signal(barrier, inc=1, device_id=(groups, sibling), device_id_type=MESH)
        pl.semaphore_wait(barrier, 1)
        c, s = cos_sin(t1_ref[pl.ds(row0, TILE), :])
        tr[...] = c
        ti[...] = s

    f = lax.broadcasted_iota(jnp.int32, (band, TILE), 0) - half + tx
    cell = lax.broadcasted_iota(jnp.int32, (band, TILE), 1) + col0
    c, s = cos_sin_int(f * (2 * cell - f), period)
    chi, clo = split(c)
    shi, slo = split(s)
    xh = jnp.concatenate(
        (jnp.concatenate((chi, shi), 1), jnp.concatenate((-shi, chi), 1)), 0
    )
    xl = jnp.concatenate(
        (jnp.concatenate((clo, slo), 1), jnp.concatenate((-slo, clo), 1)), 0
    )
    k = lax.broadcasted_iota(jnp.int32, (TILE, band), 1)
    f = jnp.where(k < half, k, half - k) + ty
    cell = lax.broadcasted_iota(jnp.int32, (TILE, band), 0) + row0
    c, s = cos_sin_int(f * (2 * cell - f), period)
    c = jnp.where(k == half, 0.0, c)
    s = jnp.where(k == half, 0.0, s)
    chi, clo = split(c)
    shi, slo = split(s)
    yh = jnp.concatenate((chi, shi), 0)
    yl = jnp.concatenate((clo, slo), 0)

    fx = (lax.broadcasted_iota(jnp.int32, (1, band), 1) - half + tx).astype(F32)
    fx2 = 9.0 * fx * fx
    k = lax.broadcasted_iota(jnp.int32, (band, 1), 0)
    fy = (jnp.where(k < half, k, half - k) + ty).astype(F32)
    keep = jnp.where(9.0 * fy * fy + fx2 < float(length * length), 1.0, 0.0).astype(BF16)
    keep = jnp.concatenate((keep, keep), 1)
    h = qh_ref[...] * keep
    l = ql_ref[...] * keep
    both = mm(jnp.concatenate((h, l), 0), xh)
    g = both[:band] + both[band:] + mm(h, xl)
    gh, gl = split(g)
    gcat[:band, :] = gh
    gcat[band : 2 * band, :] = gl
    gcat[2 * band :, :] = gh
    p = mm(jnp.concatenate((yh, yh, yl), 1), gcat[...])
    wr = p[:TILE, :TILE] - p[TILE:, TILE:]
    wi = p[:TILE, TILE:] + p[TILE:, :TILE]
    a, b = tr[...], ti[...]
    w = jnp.concatenate((wr * a - wi * b, wr * b + wi * a), 1)
    h, l = split(w)
    v = mm(h, dh[...]) + mm(l, dh[...]) + mm(h, dl[...])
    h, l = split(v)
    z = mm(drow[...], jnp.concatenate((h, l, h), 0))
    sent[step, :TILE, :] = z[:TILE, :TILE] - z[TILE:, TILE:]
    sent[step, TILE:, :] = z[:TILE, TILE:] + z[TILE:, :TILE]
    share(step).start()

    @pl.when(step == steps - 1)
    def _():
        def place(i, carry):
            for part, first in ((sent, core * steps), (got, (1 - core) * steps)):
                at = first + i
                sr[pl.ds(at, TILE, stride=beams), :] = part[i, :TILE, :]
                si[pl.ds(at, TILE, stride=beams), :] = part[i, TILE:, :]
            return carry

        def arrived(i, carry):
            share(i).wait()
            return carry

        lax.fori_loop(0, steps, arrived, 0)
        lax.fori_loop(0, steps, place, 0)
        spots = spots_ref[my_tile]
        probes = spots.shape[0]
        q = (spots[:, 0:1] + row0) * 1
        r = (spots[:, 1:2] + col0) * 1
        phase = weights[0:1, :].astype(jnp.int32) * q + weights[1:2, :].astype(jnp.int32) * r
        phase = (phase & (length - 1)).astype(F32)
        c, s = cos_sin(weights[3:4, :] - phase * (2.0 * np.pi / length))
        amp = weights[2:3, :] * (1.0 / (length * length))
        full = jnp.concatenate((c * amp, s * amp), 0)
        h = full.astype(BF16).astype(F32)
        lane = lax.broadcasted_iota(jnp.int32, full.shape, 1)
        coef = jnp.where(lane < 2 * beams, h, full - h).astype(BF16)

        def one(ky):
            at = pl.multiple_of(ky * beams, beams)
            both = jnp.concatenate((sr[pl.ds(at, beams), :], si[pl.ds(at, beams), :]), 1)
            h, l = split(both)
            e = mm(coef, jnp.concatenate((h, l, h), 0))
            er = e[:probes, :TILE] - e[probes:, TILE:]
            ei = e[:probes, TILE:] + e[probes:, :TILE]
            return er * er + ei * ei

        def mine(j, total):
            value = one(ky0 + j)
            out_ref[j] = value
            return total + value

        def others(j, total):
            return total + one((ky0 + own + j) & (TILE - 1))

        total = lax.fori_loop(0, own, mine, jnp.zeros((probes, TILE), F32), unroll=4)
        total = lax.fori_loop(0, TILE - own, others, total, unroll=4)
        level = jnp.sum(total, axis=1, keepdims=True) * (1.0 / (TILE * TILE))
        scale = 1.0 / (level + 1e-06)

        def norm(j, carry):
            out_ref[j] = out_ref[j] * scale
            return carry

        lax.fori_loop(0, own, norm, 0, unroll=4)


def per_device(potential, beam_tilts, aperture, aberration, probe_spots, crop_anchor, n):
    length = potential.shape[2]
    beams = beam_tilts.shape[0]
    per_side = CROP // TILE
    crop_rows = lax.dynamic_slice(potential[1], (0, crop_anchor[1]), (potential.shape[1], CROP))
    crop_rows = jnp.stack(
        [crop_rows[:, i * TILE : i * TILE + TILE] for i in range(CROP // TILE)]
    )
    qh, ql, t1 = forward(potential[0], crop_rows, n, length)
    own = per_side * per_side * TILE // n
    weights = jnp.concatenate(
        (beam_tilts.T.astype(F32), aperture[None], aberration[None]), 0
    )
    weights = jnp.concatenate((weights,) * 3, 1)
    dh, dl, drow = [jnp.asarray(t) for t in tile_tables()]
    probes = probe_spots.shape[1]
    smem = pl.BlockSpec(memory_space=pltpu.SMEM)
    vmem = pl.BlockSpec(memory_space=pltpu.VMEM)
    return pl.pallas_call(
        functools.partial(beam_kernel, length, beams, n),
        grid=(beams // 2,),
        out_shape=jax.ShapeDtypeStruct((own, probes, TILE), F32),
        in_specs=[smem, smem] + [vmem] * 8,
        out_specs=vmem,
        scratch_shapes=[
            pltpu.VMEM((TILE, TILE), F32),
            pltpu.VMEM((TILE, TILE), F32),
            pltpu.VMEM((3 * qh.shape[0], 2 * TILE), BF16),
            pltpu.VMEM((TILE * beams, TILE), F32),
            pltpu.VMEM((TILE * beams, TILE), F32),
            pltpu.VMEM((beams // 2, 2 * TILE, TILE), F32),
            pltpu.VMEM((beams // 2, 2 * TILE, TILE), F32),
            pltpu.SemaphoreType.DMA((beams // 2,)),
            pltpu.SemaphoreType.DMA((beams // 2,)),
        ],
        compiler_params=pltpu.CompilerParams(
            collective_id=1, has_side_effects=True, vmem_limit_bytes=LIMIT
        ),
        name="beams",
    )(beam_tilts, crop_anchor, qh, ql, t1, dh, dl, drow, probe_spots, weights)


def solution(mesh):
    placed = (P("groups", "beam", None), P(), P(), P(), P("groups", None, None), P("groups"))
    return jax.shard_map(
        functools.partial(per_device, n=mesh.shape["beam"]),
        mesh=mesh,
        in_specs=placed,
        out_specs=P(("groups", "beam"), None, None),
        check_vma=False,
    )
```

```python
import functools

import jax
import jax.numpy as jnp
import numpy as np
from jax import lax
from jax.experimental import pallas as pl
from jax.experimental.pallas import tpu as pltpu
from jax.sharding import PartitionSpec as P

CROP = 256
TILE = 128
MAX_TILT = 16
BATCH = 4
F32 = jnp.float32
BF16 = jnp.bfloat16
MESH = pl.DeviceIdType.MESH
LIMIT = 56 * 1024 * 1024


def split(value):
    high = value.astype(BF16)
    return high, (value - high.astype(F32)).astype(BF16)


def np_split(value):
    value = value.astype(np.float32)
    high = value.astype(BF16)
    return high, (value - high.astype(np.float32)).astype(BF16)


def mm(left, right):
    return jnp.dot(left, right, preferred_element_type=F32)


def polys(r):
    s = r * r
    sin = r + r * s * (-1.0 / 6 + s * (1.0 / 120 + s * (-1.0 / 5040 + s * (1.0 / 362880))))
    cos = 1.0 + s * (-0.5 + s * (1.0 / 24 + s * (-1.0 / 720 + s * (1.0 / 40320))))
    return cos, sin


def cos_sin(x):
    q = jnp.floor(x * (2.0 / np.pi) + 0.5)
    r = (x - q * 1.5703125) - q * 4.838267948966e-4
    cos, sin = polys(r)
    half = q * 0.5
    whole = jnp.floor(half)
    odd = half != whole
    c = jnp.where(odd, sin, cos)
    s = jnp.where(odd, cos, sin)
    quarter = jnp.floor(half * 0.5)
    upper = (whole - 2.0 * quarter) > 0.5
    flip_c = odd != upper
    return jnp.where(flip_c, -c, c), jnp.where(upper, -s, s)


def cos_sin_int(m, period):
    m = m & (period - 1)
    quarter = period // 4
    q = lax.shift_right_logical(
        m + quarter // 2, int(np.log2(quarter))
    )
    r = (m - q * quarter).astype(F32) * (2.0 * np.pi / period)
    cos, sin = polys(r)
    odd = (q & 1) == 1
    c = jnp.where(odd, sin, cos)
    s = jnp.where(odd, cos, sin)
    return jnp.where(((q + 1) & 2) == 2, -c, c), jnp.where((q & 2) == 2, -s, s)


def half_band(length):
    reach = int(np.sqrt((length * length - 1) // 9)) + MAX_TILT
    return -(-(reach + 1) // 64) * 64


def forward_tables(length):
    half = half_band(length)
    grid = np.arange(length)
    k = np.arange(-half, half)
    angle = 2 * np.pi / length * ((grid[:, None] * k[None, :]) % length)
    c, s = np.cos(angle), np.sin(angle)
    cols = np.concatenate(
        (np.concatenate((c, -s), 1), np.concatenate((s, c), 1)), 0
    )
    k = np.arange(half)
    angle = 2 * np.pi / length * ((k[:, None] * grid[None, :]) % length)
    rows = np.concatenate((np.cos(angle), np.sin(angle)), 0)
    return np_split(cols) + np_split(rows)


def forward_kernel(
    n, remote, own_ref, ch_any, cl_any, rh_any, rl_any, qh_ref, ql_ref, *rest
):
    if remote:
        t1_ref, buf, ch, cl, rh, rl, th, tl, uh, ul, tab_sem, send_sem, recv_sem = rest
    else:
        ch, cl, rh, rl, th, tl, uh, ul, tab_sem = rest
    pairs = ((ch_any, ch), (cl_any, cl), (rh_any, rh), (rl_any, rl))
    tables = [
        pltpu.make_async_copy(src, dst, tab_sem.at[i]) for i, (src, dst) in enumerate(pairs)
    ]
    for copy in tables:
        copy.start()
    length = th.shape[0]
    half = rh.shape[0] // 2
    band = 2 * half

    def transmit(value, row, count):
        c, s = cos_sin(value)
        h, l = split(c)
        th[pl.ds(row, count), :length] = h
        tl[pl.ds(row, count), :length] = l
        h, l = split(s)
        th[pl.ds(row, count), length:] = h
        tl[pl.ds(row, count), length:] = l

    if remote:
        rows = own_ref.shape[1]
        groups = lax.axis_index("groups")
        me = lax.axis_index("beam")
        planes = n // 4
        plane, low = me // 4, me % 4
        across = plane * 4 + (low + 2) % 4
        sibling = plane * 4 + (low // 2) * 2 + (1 - low % 2)

        def peer(step):
            return ((plane + step) % planes) * 4 + low

        barrier = pltpu.get_barrier_semaphore()
        friends = [across, sibling] + [peer(step) for step in range(1, planes)]
        for friend in friends:
            pl.semaphore_signal(barrier, inc=1, device_id=(groups, friend), device_id_type=MESH)
        pl.semaphore_wait(barrier, len(friends))

        def push(src, block, target, index):
            return pltpu.make_async_remote_copy(
                src_ref=src,
                dst_ref=buf.at[block],
                send_sem=send_sem.at[index],
                recv_sem=recv_sem.at[block],
                device_id=(groups, target),
                device_id_type=MESH,
            )

        def own_part(target):
            return own_ref.at[(target // 4) % (CROP // TILE)]

        started = []

        def go(src, block, target):
            copy = push(src, block, target, len(started))
            copy.start()
            started.append(copy)

        def arrive(block):
            push(own_part(me), block, sibling, 0).wait_recv()

        def work(block, ref):
            at = pl.multiple_of(block * rows, rows)
            transmit(ref[:, :length], at, rows)
            t1_ref[pl.ds(at, rows), :] = ref[:, length:]

        order = [1, planes - 1] + list(range(2, planes - 1))
        order = [s for i, s in enumerate(order) if s not in order[:i]]
        go(own_part(me), me, across)
        for step in order:
            go(own_part(peer(step)), me, peer(step))
        go(own_part(me), me, sibling)
        work(me, own_part(me))
        for step in [0] + order:
            base = ((plane + step) % planes) * 4
            if step != 0:
                block = base + low
                arrive(block)
                go(buf.at[block], block, across)
                go(buf.at[block], block, sibling)
                work(block, buf.at[block])
            block = base + (low + 2) % 4
            arrive(block)
            go(buf.at[block], block, sibling)
            work(block, buf.at[block])
        for step in [0] + order:
            base = ((plane + step) % planes) * 4
            for block in (
                base + (low // 2) * 2 + (1 - low % 2),
                base + (1 - low // 2) * 2 + (1 - low % 2),
            ):
                arrive(block)
                work(block, buf.at[block])
    else:
        transmit(own_ref[...], 0, length)

    for copy in tables:
        copy.wait()

    step_rows = 256

    def stage_one(i, carry):
        at = pl.multiple_of(i * step_rows, step_rows)
        h = th[pl.ds(at, step_rows), :]
        l = tl[pl.ds(at, step_rows), :]
        u = mm(h, ch[...]) + mm(l, ch[...]) + mm(h, cl[...])
        high, lower = split(u)
        uh[pl.ds(at, step_rows), :] = high
        ul[pl.ds(at, step_rows), :] = lower
        return carry

    lax.fori_loop(0, length // step_rows, stage_one, 0)
    for j in range(band // 128):
        a, b = slice(j * 128, j * 128 + 128), slice(band + j * 128, band + j * 128 + 128)
        h = jnp.concatenate((uh[:, a], uh[:, b]), 1)
        l = jnp.concatenate((ul[:, a], ul[:, b]), 1)
        p = mm(rh[...], h) + mm(rh[...], l) + mm(rl[...], h)
        cr, ci, sr, si = p[:half, :128], p[:half, 128:], p[half:, :128], p[half:, 128:]
        for at, real, imag in ((0, cr + si, ci - sr), (half, cr - si, ci + sr)):
            h, l = split(real)
            qh_ref[at : at + half, a] = h
            ql_ref[at : at + half, a] = l
            h, l = split(imag)
            qh_ref[at : at + half, b] = h
            ql_ref[at : at + half, b] = l
    if remote:
        for copy in started:
            copy.wait_send()


def forward(own, crop, n, length):
    rows = own.shape[0]
    half = half_band(length)
    band = 2 * half
    remote = rows % 16 == 0 and n == 4 * (CROP // TILE) ** 2
    tables = [jnp.asarray(t) for t in forward_tables(length)]
    vmem = pl.BlockSpec(memory_space=pltpu.VMEM)
    scratch = [
        pltpu.VMEM((2 * length, 2 * band), BF16),
        pltpu.VMEM((2 * length, 2 * band), BF16),
        pltpu.VMEM((band, length), BF16),
        pltpu.VMEM((band, length), BF16),
        pltpu.VMEM((length, 2 * length), BF16),
        pltpu.VMEM((length, 2 * length), BF16),
        pltpu.VMEM((length, 2 * band), BF16),
        pltpu.VMEM((length, 2 * band), BF16),
        pltpu.SemaphoreType.DMA((4,)),
    ]
    outs = [jax.ShapeDtypeStruct((band, 2 * band), BF16)] * 2
    if remote:
        outs = outs + [jax.ShapeDtypeStruct((length, TILE), F32)]
        scratch = (
            [pltpu.VMEM((n, rows, length + TILE), F32)]
            + scratch
            + [pltpu.SemaphoreType.DMA((n,))] * 2
        )
        own = jnp.stack([jnp.concatenate((own, part), 1) for part in crop])
        params = pltpu.CompilerParams(
            collective_id=0, has_side_effects=True, vmem_limit_bytes=LIMIT
        )
    else:
        own = lax.all_gather(own, "beam", axis=0, tiled=True)
        params = pltpu.CompilerParams(vmem_limit_bytes=LIMIT)
    result = pl.pallas_call(
        functools.partial(forward_kernel, n, remote),
        out_shape=outs,
        in_specs=[vmem] + [pl.BlockSpec(memory_space=pl.ANY)] * 4,
        out_specs=[vmem] * len(outs),
        scratch_shapes=scratch,
        compiler_params=params,
        name="forward",
    )(own, *tables)
    if remote:
        return result
    tile = lax.axis_index("beam") * (CROP // TILE) ** 2 // n
    crop = lax.dynamic_index_in_dim(
        lax.all_gather(crop, "beam", axis=1, tiled=True), tile % (CROP // TILE), 0, False
    )
    return (*result, crop)


def tile_tables():
    k = np.arange(TILE)
    angle = 2 * np.pi / TILE * ((k[:, None] * k[None, :]) % TILE)
    c, s = np.cos(angle), np.sin(angle)
    cols = np.concatenate((np.concatenate((c, -s), 1), np.concatenate((s, c), 1)), 0)
    rh, rl = np_split(np.concatenate((c, -s), 0))
    return np_split(cols) + (np.concatenate((rh, rh, rl), 1),)


def beam_kernel(
    length, beams, n, tilts, anchor, qh_ref, ql_ref, t1_ref, dh, dl, drow, spots_ref, weights,
    out_ref, coef, tr, ti, gcat, sr, si, sent, got, send_sem, recv_sem,
):
    step = pl.program_id(0)
    steps = beams // 2
    groups = lax.axis_index("groups")
    me = lax.axis_index("beam")
    core = me % 2
    sibling = me + 1 - 2 * core
    beam = core * steps + step
    own = out_ref.shape[0]
    per_side = CROP // TILE
    my_tile = me * own // TILE
    ky0 = me * own % TILE
    col_at = pl.multiple_of((my_tile % per_side) * TILE, TILE)
    row0 = anchor[0] + TILE * (my_tile // per_side)
    col0 = anchor[1] + col_at
    band = qh_ref.shape[0]
    half = band // 2
    ty, tx = tilts[0, beam], tilts[1, beam]
    period = 2 * length

    def share(at):
        return pltpu.make_async_remote_copy(
            src_ref=sent.at[at],
            dst_ref=got.at[at],
            send_sem=send_sem.at[at],
            recv_sem=recv_sem.at[at],
            device_id=(groups, sibling),
            device_id_type=MESH,
        )

    @pl.when(step == 0)
    def _():
        barrier = pltpu.get_barrier_semaphore()
        pl.semaphore_signal(barrier, inc=1, device_id=(groups, sibling), device_id_type=MESH)
        pl.semaphore_wait(barrier, 1)
        c, s = cos_sin(t1_ref[pl.ds(row0, TILE), :])
        tr[...] = c
        ti[...] = s

    f = lax.broadcasted_iota(jnp.int32, (band, TILE), 0) - half + tx
    cell = lax.broadcasted_iota(jnp.int32, (band, TILE), 1) + col0
    c, s = cos_sin_int(f * (2 * cell - f), period)
    chi, clo = split(c)
    shi, slo = split(s)
    xh = jnp.concatenate(
        (jnp.concatenate((chi, shi), 1), jnp.concatenate((-shi, chi), 1)), 0
    )
    xl = jnp.concatenate(
        (jnp.concatenate((clo, slo), 1), jnp.concatenate((-slo, clo), 1)), 0
    )
    k = lax.broadcasted_iota(jnp.int32, (TILE, band), 1)
    f = jnp.where(k < half, k, half - k) + ty
    cell = lax.broadcasted_iota(jnp.int32, (TILE, band), 0) + row0
    c, s = cos_sin_int(f * (2 * cell - f), period)
    c = jnp.where(k == half, 0.0, c)
    s = jnp.where(k == half, 0.0, s)
    chi, clo = split(c)
    shi, slo = split(s)
    yh = jnp.concatenate((chi, shi), 0)
    yl = jnp.concatenate((clo, slo), 0)

    fx = (lax.broadcasted_iota(jnp.int32, (1, band), 1) - half + tx).astype(F32)
    fx2 = 9.0 * fx * fx
    k = lax.broadcasted_iota(jnp.int32, (band, 1), 0)
    fy = (jnp.where(k < half, k, half - k) + ty).astype(F32)
    keep = jnp.where(9.0 * fy * fy + fx2 < float(length * length), 1.0, 0.0).astype(BF16)
    keep = jnp.concatenate((keep, keep), 1)
    h = qh_ref[...] * keep
    l = ql_ref[...] * keep
    both = mm(jnp.concatenate((h, l), 0), xh)
    g = both[:band] + both[band:] + mm(h, xl)
    gh, gl = split(g)
    gcat[:band, :] = gh
    gcat[band : 2 * band, :] = gl
    gcat[2 * band :, :] = gh
    p = mm(jnp.concatenate((yh, yh, yl), 1), gcat[...])
    wr = p[:TILE, :TILE] - p[TILE:, TILE:]
    wi = p[:TILE, TILE:] + p[TILE:, :TILE]
    a, b = tr[...], ti[...]
    w = jnp.concatenate((wr * a - wi * b, wr * b + wi * a), 1)
    h, l = split(w)
    v = mm(h, dh[...]) + mm(l, dh[...]) + mm(h, dl[...])
    h, l = split(v)
    z = mm(drow[...], jnp.concatenate((h, l, h), 0))
    sent[step, :TILE, :] = z[:TILE, :TILE] - z[TILE:, TILE:]
    sent[step, TILE:, :] = z[:TILE, TILE:] + z[TILE:, :TILE]
    share(step).start()

    @pl.when(step == steps - 1)
    def _():
        def place(i, carry):
            for part, first in ((sent, core * steps), (got, (1 - core) * steps)):
                at = first + i
                sr[pl.ds(at, TILE, stride=beams), :] = part[i, :TILE, :]
                si[pl.ds(at, TILE, stride=beams), :] = part[i, TILE:, :]
            return carry

        def arrived(i, carry):
            share(i).wait()
            return carry

        lax.fori_loop(0, steps, arrived, 0)
        lax.fori_loop(0, steps, place, 0)
        spots = spots_ref[my_tile]
        probes = spots.shape[0]
        q = (spots[:, 0:1] + row0) * 1
        r = (spots[:, 1:2] + col0) * 1
        phase = weights[0:1, :].astype(jnp.int32) * q + weights[1:2, :].astype(jnp.int32) * r
        phase = (phase & (length - 1)).astype(F32)
        c, s = cos_sin(weights[3:4, :] - phase * (2.0 * np.pi / length))
        amp = weights[2:3, :] * (1.0 / (length * length))
        full = jnp.concatenate((c * amp, s * amp), 0)
        h = full.astype(BF16).astype(F32)
        lane = lax.broadcasted_iota(jnp.int32, full.shape, 1)
        mixed = jnp.where(lane < 2 * BATCH * beams, h, full - h)
        slot = lax.rem(lax.div(lane, beams), BATCH)
        for i in range(BATCH):
            coef[2 * probes * i : 2 * probes * (i + 1), :] = jnp.where(
                slot == i, mixed, 0.0
            ).astype(BF16)

        def several(ky):
            at = pl.multiple_of(ky * beams, BATCH * beams)
            count = BATCH * beams
            both = jnp.concatenate((sr[pl.ds(at, count), :], si[pl.ds(at, count), :]), 1)
            h, l = split(both)
            e = mm(coef[...], jnp.concatenate((h, l, h), 0))
            found = []
            for i in range(BATCH):
                a = e[2 * probes * i : 2 * probes * i + probes]
                b = e[2 * probes * i + probes : 2 * probes * (i + 1)]
                er = a[:, :TILE] - b[:, TILE:]
                ei = a[:, TILE:] + b[:, :TILE]
                found.append(er * er + ei * ei)
            return found

        def mine(j, total):
            values = several(ky0 + j * BATCH)
            for i, value in enumerate(values):
                out_ref[j * BATCH + i] = value
            return total + ((values[0] + values[1]) + (values[2] + values[3]))

        def others(j, total):
            values = several((ky0 + own + j * BATCH) & (TILE - 1))
            return total + ((values[0] + values[1]) + (values[2] + values[3]))

        total = jnp.zeros((probes, TILE), F32)
        total = lax.fori_loop(0, own // BATCH, mine, total, unroll=min(4, own // BATCH))
        total = lax.fori_loop(0, (TILE - own) // BATCH, others, total, unroll=4)
        level = jnp.sum(total, axis=1, keepdims=True) * (1.0 / (TILE * TILE))
        scale = 1.0 / (level + 1e-06)

        def norm(j, carry):
            out_ref[j] = out_ref[j] * scale
            return carry

        lax.fori_loop(0, own, norm, 0, unroll=4)


def per_device(potential, beam_tilts, aperture, aberration, probe_spots, crop_anchor, n):
    length = potential.shape[2]
    beams = beam_tilts.shape[0]
    per_side = CROP // TILE
    crop_rows = lax.dynamic_slice(potential[1], (0, crop_anchor[1]), (potential.shape[1], CROP))
    crop_rows = jnp.stack(
        [crop_rows[:, i * TILE : i * TILE + TILE] for i in range(CROP // TILE)]
    )
    qh, ql, t1 = forward(potential[0], crop_rows, n, length)
    own = per_side * per_side * TILE // n
    weights = jnp.concatenate(
        (beam_tilts.T.astype(F32), aperture[None], aberration[None]), 0
    )
    weights = jnp.concatenate((weights,) * (3 * BATCH), 1)
    dh, dl, drow = [jnp.asarray(t) for t in tile_tables()]
    probes = probe_spots.shape[1]
    smem = pl.BlockSpec(memory_space=pltpu.SMEM)
    vmem = pl.BlockSpec(memory_space=pltpu.VMEM)
    return pl.pallas_call(
        functools.partial(beam_kernel, length, beams, n),
        grid=(beams // 2,),
        out_shape=jax.ShapeDtypeStruct((own, probes, TILE), F32),
        in_specs=[smem, smem] + [vmem] * 8,
        out_specs=vmem,
        scratch_shapes=[
            pltpu.VMEM((2 * BATCH * probes, 3 * BATCH * beams), BF16),
            pltpu.VMEM((TILE, TILE), F32),
            pltpu.VMEM((TILE, TILE), F32),
            pltpu.VMEM((3 * qh.shape[0], 2 * TILE), BF16),
            pltpu.VMEM((TILE * beams, TILE), F32),
            pltpu.VMEM((TILE * beams, TILE), F32),
            pltpu.VMEM((beams // 2, 2 * TILE, TILE), F32),
            pltpu.VMEM((beams // 2, 2 * TILE, TILE), F32),
            pltpu.SemaphoreType.DMA((beams // 2,)),
            pltpu.SemaphoreType.DMA((beams // 2,)),
        ],
        compiler_params=pltpu.CompilerParams(
            collective_id=1, has_side_effects=True, vmem_limit_bytes=LIMIT
        ),
        name="beams",
    )(beam_tilts.T, crop_anchor, qh, ql, t1, dh, dl, drow, probe_spots, weights)


def solution(mesh):
    placed = (P("groups", "beam", None), P(), P(), P(), P("groups", None, None), P("groups"))
    return jax.shard_map(
        functools.partial(per_device, n=mesh.shape["beam"]),
        mesh=mesh,
        in_specs=placed,
        out_specs=P(("groups", "beam"), None, None),
        check_vma=False,
    )
```

```python
import functools

import jax
import jax.numpy as jnp
import numpy as np
from jax import lax
from jax.experimental import pallas as pl
from jax.experimental.pallas import tpu as pltpu
from jax.sharding import PartitionSpec as P

CROP = 256
TILE = 128
MAX_TILT = 16
BATCH = 4
PAIR = 2
F32 = jnp.float32
BF16 = jnp.bfloat16
MESH = pl.DeviceIdType.MESH
LIMIT = 56 * 1024 * 1024


def split(value):
    high = value.astype(BF16)
    return high, (value - high.astype(F32)).astype(BF16)


def np_split(value):
    value = value.astype(np.float32)
    high = value.astype(BF16)
    return high, (value - high.astype(np.float32)).astype(BF16)


def mm(left, right):
    return jnp.dot(left, right, preferred_element_type=F32)


def polys(r):
    s = r * r
    sin = r + r * s * (-1.0 / 6 + s * (1.0 / 120 + s * (-1.0 / 5040 + s * (1.0 / 362880))))
    cos = 1.0 + s * (-0.5 + s * (1.0 / 24 + s * (-1.0 / 720 + s * (1.0 / 40320))))
    return cos, sin


def cos_sin(x):
    q = jnp.floor(x * (2.0 / np.pi) + 0.5)
    r = (x - q * 1.5703125) - q * 4.838267948966e-4
    cos, sin = polys(r)
    half = q * 0.5
    whole = jnp.floor(half)
    odd = half != whole
    c = jnp.where(odd, sin, cos)
    s = jnp.where(odd, cos, sin)
    quarter = jnp.floor(half * 0.5)
    upper = (whole - 2.0 * quarter) > 0.5
    flip_c = odd != upper
    return jnp.where(flip_c, -c, c), jnp.where(upper, -s, s)


def cos_sin_int(m, period):
    m = m & (period - 1)
    quarter = period // 4
    q = lax.shift_right_logical(
        m + quarter // 2, int(np.log2(quarter))
    )
    r = (m - q * quarter).astype(F32) * (2.0 * np.pi / period)
    cos, sin = polys(r)
    odd = (q & 1) == 1
    c = jnp.where(odd, sin, cos)
    s = jnp.where(odd, cos, sin)
    return jnp.where(((q + 1) & 2) == 2, -c, c), jnp.where((q & 2) == 2, -s, s)


def half_band(length):
    reach = int(np.sqrt((length * length - 1) // 9)) + MAX_TILT
    return -(-(reach + 1) // 64) * 64


def forward_tables(length):
    half = half_band(length)
    grid = np.arange(length)
    k = np.arange(-half, half)
    angle = 2 * np.pi / length * ((grid[:, None] * k[None, :]) % length)
    c, s = np.cos(angle), np.sin(angle)
    cols = np.concatenate(
        (np.concatenate((c, -s), 1), np.concatenate((s, c), 1)), 0
    )
    k = np.arange(half)
    angle = 2 * np.pi / length * ((k[:, None] * grid[None, :]) % length)
    rows = np.concatenate((np.cos(angle), np.sin(angle)), 0)
    return np_split(cols) + np_split(rows)


def forward_kernel(
    n, remote, own_ref, ch_any, cl_any, rh_any, rl_any, qh_ref, ql_ref, *rest
):
    if remote:
        t1_ref, buf, ch, cl, rh, rl, th, tl, uh, ul, tab_sem, send_sem, recv_sem = rest
    else:
        ch, cl, rh, rl, th, tl, uh, ul, tab_sem = rest
    pairs = ((ch_any, ch), (cl_any, cl), (rh_any, rh), (rl_any, rl))
    tables = [
        pltpu.make_async_copy(src, dst, tab_sem.at[i]) for i, (src, dst) in enumerate(pairs)
    ]
    for copy in tables:
        copy.start()
    length = th.shape[0]
    half = rh.shape[0] // 2
    band = 2 * half

    def transmit(value, row, count):
        c, s = cos_sin(value)
        h, l = split(c)
        th[pl.ds(row, count), :length] = h
        tl[pl.ds(row, count), :length] = l
        h, l = split(s)
        th[pl.ds(row, count), length:] = h
        tl[pl.ds(row, count), length:] = l

    if remote:
        rows = own_ref.shape[1]
        groups = lax.axis_index("groups")
        me = lax.axis_index("beam")
        planes = n // 4
        plane, low = me // 4, me % 4
        across = plane * 4 + (low + 2) % 4
        sibling = plane * 4 + (low // 2) * 2 + (1 - low % 2)

        def peer(step):
            return ((plane + step) % planes) * 4 + low

        barrier = pltpu.get_barrier_semaphore()
        friends = [across, sibling] + [peer(step) for step in range(1, planes)]
        for friend in friends:
            pl.semaphore_signal(barrier, inc=1, device_id=(groups, friend), device_id_type=MESH)
        pl.semaphore_wait(barrier, len(friends))

        def push(src, block, target, index):
            return pltpu.make_async_remote_copy(
                src_ref=src,
                dst_ref=buf.at[block],
                send_sem=send_sem.at[index],
                recv_sem=recv_sem.at[block],
                device_id=(groups, target),
                device_id_type=MESH,
            )

        def own_part(target):
            return own_ref.at[(target // 4) % (CROP // TILE)]

        started = []

        def go(src, block, target):
            copy = push(src, block, target, len(started))
            copy.start()
            started.append(copy)

        def arrive(block):
            push(own_part(me), block, sibling, 0).wait_recv()

        def work(block, ref):
            at = pl.multiple_of(block * rows, rows)
            transmit(ref[:, :length], at, rows)
            t1_ref[pl.ds(at, rows), :] = ref[:, length:]

        order = [1, planes - 1] + list(range(2, planes - 1))
        order = [s for i, s in enumerate(order) if s not in order[:i]]
        go(own_part(me), me, across)
        for step in order:
            go(own_part(peer(step)), me, peer(step))
        go(own_part(me), me, sibling)
        work(me, own_part(me))
        for step in [0] + order:
            base = ((plane + step) % planes) * 4
            if step != 0:
                block = base + low
                arrive(block)
                go(buf.at[block], block, across)
                go(buf.at[block], block, sibling)
                work(block, buf.at[block])
            block = base + (low + 2) % 4
            arrive(block)
            go(buf.at[block], block, sibling)
            work(block, buf.at[block])
        for step in [0] + order:
            base = ((plane + step) % planes) * 4
            for block in (
                base + (low // 2) * 2 + (1 - low % 2),
                base + (1 - low // 2) * 2 + (1 - low % 2),
            ):
                arrive(block)
                work(block, buf.at[block])
    else:
        transmit(own_ref[...], 0, length)

    for copy in tables:
        copy.wait()

    step_rows = 256

    def stage_one(i, carry):
        at = pl.multiple_of(i * step_rows, step_rows)
        h = th[pl.ds(at, step_rows), :]
        l = tl[pl.ds(at, step_rows), :]
        u = mm(h, ch[...]) + mm(l, ch[...]) + mm(h, cl[...])
        high, lower = split(u)
        uh[pl.ds(at, step_rows), :] = high
        ul[pl.ds(at, step_rows), :] = lower
        return carry

    lax.fori_loop(0, length // step_rows, stage_one, 0)
    for j in range(band // 128):
        a, b = slice(j * 128, j * 128 + 128), slice(band + j * 128, band + j * 128 + 128)
        h = jnp.concatenate((uh[:, a], uh[:, b]), 1)
        l = jnp.concatenate((ul[:, a], ul[:, b]), 1)
        p = mm(rh[...], h) + mm(rh[...], l) + mm(rl[...], h)
        cr, ci, sr, si = p[:half, :128], p[:half, 128:], p[half:, :128], p[half:, 128:]
        for at, real, imag in ((0, cr + si, ci - sr), (half, cr - si, ci + sr)):
            h, l = split(real)
            qh_ref[at : at + half, a] = h
            ql_ref[at : at + half, a] = l
            h, l = split(imag)
            qh_ref[at : at + half, b] = h
            ql_ref[at : at + half, b] = l
    if remote:
        for copy in started:
            copy.wait_send()


def forward(own, crop, n, length):
    rows = own.shape[0]
    half = half_band(length)
    band = 2 * half
    remote = rows % 16 == 0 and n == 4 * (CROP // TILE) ** 2
    tables = [jnp.asarray(t) for t in forward_tables(length)]
    vmem = pl.BlockSpec(memory_space=pltpu.VMEM)
    scratch = [
        pltpu.VMEM((2 * length, 2 * band), BF16),
        pltpu.VMEM((2 * length, 2 * band), BF16),
        pltpu.VMEM((band, length), BF16),
        pltpu.VMEM((band, length), BF16),
        pltpu.VMEM((length, 2 * length), BF16),
        pltpu.VMEM((length, 2 * length), BF16),
        pltpu.VMEM((length, 2 * band), BF16),
        pltpu.VMEM((length, 2 * band), BF16),
        pltpu.SemaphoreType.DMA((4,)),
    ]
    outs = [jax.ShapeDtypeStruct((band, 2 * band), BF16)] * 2
    if remote:
        outs = outs + [jax.ShapeDtypeStruct((length, TILE), F32)]
        scratch = (
            [pltpu.VMEM((n, rows, length + TILE), F32)]
            + scratch
            + [pltpu.SemaphoreType.DMA((n,))] * 2
        )
        own = jnp.stack([jnp.concatenate((own, part), 1) for part in crop])
        params = pltpu.CompilerParams(
            collective_id=0, has_side_effects=True, vmem_limit_bytes=LIMIT
        )
    else:
        own = lax.all_gather(own, "beam", axis=0, tiled=True)
        params = pltpu.CompilerParams(vmem_limit_bytes=LIMIT)
    result = pl.pallas_call(
        functools.partial(forward_kernel, n, remote),
        out_shape=outs,
        in_specs=[vmem] + [pl.BlockSpec(memory_space=pl.ANY)] * 4,
        out_specs=[vmem] * len(outs),
        scratch_shapes=scratch,
        compiler_params=params,
        name="forward",
    )(own, *tables)
    if remote:
        return result
    tile = lax.axis_index("beam") * (CROP // TILE) ** 2 // n
    crop = lax.dynamic_index_in_dim(
        lax.all_gather(crop, "beam", axis=1, tiled=True), tile % (CROP // TILE), 0, False
    )
    return (*result, crop)


def tile_tables():
    k = np.arange(TILE)
    angle = 2 * np.pi / TILE * ((k[:, None] * k[None, :]) % TILE)
    c, s = np.cos(angle), np.sin(angle)
    cols = np.concatenate((np.concatenate((c, -s), 1), np.concatenate((s, c), 1)), 0)
    rh, rl = np_split(np.concatenate((c, -s), 0))
    return np_split(cols) + (np.concatenate((rh, rh, rl), 1),)


def beam_kernel(
    length, beams, n, tilts, anchor, qh_ref, ql_ref, t1_ref, dh, dl, drow, spots_ref, weights,
    out_ref, coef, tr, ti, gcats, sr, si, sent, got, send_sem, recv_sem,
):
    step = pl.program_id(0)
    steps = beams // 2
    groups = lax.axis_index("groups")
    me = lax.axis_index("beam")
    core = me % 2
    sibling = me + 1 - 2 * core
    own = out_ref.shape[0]
    per_side = CROP // TILE
    my_tile = me * own // TILE
    ky0 = me * own % TILE
    col_at = pl.multiple_of((my_tile % per_side) * TILE, TILE)
    row0 = anchor[0] + TILE * (my_tile // per_side)
    col0 = anchor[1] + col_at
    band = qh_ref.shape[0]
    half = band // 2
    period = 2 * length

    def share(at):
        return pltpu.make_async_remote_copy(
            src_ref=sent.at[at],
            dst_ref=got.at[at],
            send_sem=send_sem.at[at],
            recv_sem=recv_sem.at[at],
            device_id=(groups, sibling),
            device_id_type=MESH,
        )

    @pl.when(step == 0)
    def _():
        barrier = pltpu.get_barrier_semaphore()
        pl.semaphore_signal(barrier, inc=1, device_id=(groups, sibling), device_id_type=MESH)
        pl.semaphore_wait(barrier, 1)
        c, s = cos_sin(t1_ref[pl.ds(row0, TILE), :])
        tr[...] = c
        ti[...] = s

    def one_beam(index, gcat):
        beam = core * steps + index
        ty, tx = tilts[0, beam], tilts[1, beam]
        f = lax.broadcasted_iota(jnp.int32, (band, TILE), 0) - half + tx
        cell = lax.broadcasted_iota(jnp.int32, (band, TILE), 1) + col0
        c, s = cos_sin_int(f * (2 * cell - f), period)
        chi, clo = split(c)
        shi, slo = split(s)
        xh = jnp.concatenate(
            (jnp.concatenate((chi, shi), 1), jnp.concatenate((-shi, chi), 1)), 0
        )
        xl = jnp.concatenate(
            (jnp.concatenate((clo, slo), 1), jnp.concatenate((-slo, clo), 1)), 0
        )
        k = lax.broadcasted_iota(jnp.int32, (TILE, band), 1)
        f = jnp.where(k < half, k, half - k) + ty
        cell = lax.broadcasted_iota(jnp.int32, (TILE, band), 0) + row0
        c, s = cos_sin_int(f * (2 * cell - f), period)
        c = jnp.where(k == half, 0.0, c)
        s = jnp.where(k == half, 0.0, s)
        chi, clo = split(c)
        shi, slo = split(s)
        yh = jnp.concatenate((chi, shi), 0)
        yl = jnp.concatenate((clo, slo), 0)

        fx = (lax.broadcasted_iota(jnp.int32, (1, band), 1) - half + tx).astype(F32)
        fx2 = 9.0 * fx * fx
        k = lax.broadcasted_iota(jnp.int32, (band, 1), 0)
        fy = (jnp.where(k < half, k, half - k) + ty).astype(F32)
        keep = jnp.where(9.0 * fy * fy + fx2 < float(length * length), 1.0, 0.0).astype(BF16)
        keep = jnp.concatenate((keep, keep), 1)
        h = qh_ref[...] * keep
        l = ql_ref[...] * keep
        both = mm(jnp.concatenate((h, l), 0), xh)
        g = both[:band] + both[band:] + mm(h, xl)
        gh, gl = split(g)
        gcat[:band, :] = gh
        gcat[band : 2 * band, :] = gl
        gcat[2 * band :, :] = gh
        p = mm(jnp.concatenate((yh, yh, yl), 1), gcat[...])
        wr = p[:TILE, :TILE] - p[TILE:, TILE:]
        wi = p[:TILE, TILE:] + p[TILE:, :TILE]
        a, b = tr[...], ti[...]
        w = jnp.concatenate((wr * a - wi * b, wr * b + wi * a), 1)
        h, l = split(w)
        v = mm(h, dh[...]) + mm(l, dh[...]) + mm(h, dl[...])
        h, l = split(v)
        z = mm(drow[...], jnp.concatenate((h, l, h), 0))
        sent[index, :TILE, :] = z[:TILE, :TILE] - z[TILE:, TILE:]
        sent[index, TILE:, :] = z[:TILE, TILE:] + z[TILE:, :TILE]
        share(index).start()

    for i in range(PAIR):
        one_beam(step * PAIR + i, gcats.at[i])

    @pl.when(step == steps // PAIR - 1)
    def _():
        def place(i, carry):
            for part, first in ((sent, core * steps), (got, (1 - core) * steps)):
                at = first + i
                sr[pl.ds(at, TILE, stride=beams), :] = part[i, :TILE, :]
                si[pl.ds(at, TILE, stride=beams), :] = part[i, TILE:, :]
            return carry

        def arrived(i, carry):
            share(i).wait()
            return carry

        lax.fori_loop(0, steps, arrived, 0)
        lax.fori_loop(0, steps, place, 0)
        spots = spots_ref[my_tile].astype(F32)
        probes = spots.shape[1]
        eye = lax.broadcasted_iota(jnp.int32, (probes, probes), 0) == lax.broadcasted_iota(
            jnp.int32, (probes, probes), 1
        )

        def column(line):
            picked = jnp.where(eye, jnp.broadcast_to(line, (probes, probes)), 0.0)
            return jnp.sum(picked, axis=1, keepdims=True).astype(jnp.int32)

        q = column(spots[0:1, :]) + row0
        r = column(spots[1:2, :]) + col0
        phase = weights[0:1, :].astype(jnp.int32) * q + weights[1:2, :].astype(jnp.int32) * r
        phase = (phase & (length - 1)).astype(F32)
        c, s = cos_sin(weights[3:4, :] - phase * (2.0 * np.pi / length))
        amp = weights[2:3, :] * (1.0 / (length * length))
        full = jnp.concatenate((c * amp, s * amp), 0)
        h = full.astype(BF16).astype(F32)
        lane = lax.broadcasted_iota(jnp.int32, full.shape, 1)
        mixed = jnp.where(lane < 2 * BATCH * beams, h, full - h)
        slot = lax.rem(lax.div(lane, beams), BATCH)
        for i in range(BATCH):
            coef[2 * probes * i : 2 * probes * (i + 1), :] = jnp.where(
                slot == i, mixed, 0.0
            ).astype(BF16)

        def several(ky):
            at = pl.multiple_of(ky * beams, BATCH * beams)
            count = BATCH * beams
            both = jnp.concatenate((sr[pl.ds(at, count), :], si[pl.ds(at, count), :]), 1)
            h, l = split(both)
            e = mm(coef[...], jnp.concatenate((h, l, h), 0))
            found = []
            for i in range(BATCH):
                a = e[2 * probes * i : 2 * probes * i + probes]
                b = e[2 * probes * i + probes : 2 * probes * (i + 1)]
                er = a[:, :TILE] - b[:, TILE:]
                ei = a[:, TILE:] + b[:, :TILE]
                found.append(er * er + ei * ei)
            return found

        def mine(j, total):
            values = several(ky0 + j * BATCH)
            for i, value in enumerate(values):
                out_ref[j * BATCH + i] = value
            return total + ((values[0] + values[1]) + (values[2] + values[3]))

        def others(j, total):
            values = several((ky0 + own + j * BATCH) & (TILE - 1))
            return total + ((values[0] + values[1]) + (values[2] + values[3]))

        total = jnp.zeros((probes, TILE), F32)
        total = lax.fori_loop(0, own // BATCH, mine, total, unroll=min(4, own // BATCH))
        total = lax.fori_loop(0, (TILE - own) // BATCH, others, total, unroll=4)
        level = jnp.sum(total, axis=1, keepdims=True) * (1.0 / (TILE * TILE))
        scale = 1.0 / (level + 1e-06)

        def norm(j, carry):
            out_ref[j] = out_ref[j] * scale
            return carry

        lax.fori_loop(0, own, norm, 0, unroll=4)


def per_device(potential, beam_tilts, aperture, aberration, probe_spots, crop_anchor, n):
    length = potential.shape[2]
    beams = beam_tilts.shape[0]
    per_side = CROP // TILE
    crop_rows = lax.dynamic_slice(potential[1], (0, crop_anchor[1]), (potential.shape[1], CROP))
    crop_rows = jnp.stack(
        [crop_rows[:, i * TILE : i * TILE + TILE] for i in range(CROP // TILE)]
    )
    qh, ql, t1 = forward(potential[0], crop_rows, n, length)
    own = per_side * per_side * TILE // n
    weights = jnp.concatenate(
        (beam_tilts.T.astype(F32), aperture[None], aberration[None]), 0
    )
    weights = jnp.concatenate((weights,) * (3 * BATCH), 1)
    dh, dl, drow = [jnp.asarray(t) for t in tile_tables()]
    probes = probe_spots.shape[1]
    smem = pl.BlockSpec(memory_space=pltpu.SMEM)
    vmem = pl.BlockSpec(memory_space=pltpu.VMEM)
    return pl.pallas_call(
        functools.partial(beam_kernel, length, beams, n),
        grid=(beams // 2 // PAIR,),
        out_shape=jax.ShapeDtypeStruct((own, probes, TILE), F32),
        in_specs=[smem, smem] + [vmem] * 8,
        out_specs=vmem,
        scratch_shapes=[
            pltpu.VMEM((2 * BATCH * probes, 3 * BATCH * beams), BF16),
            pltpu.VMEM((TILE, TILE), F32),
            pltpu.VMEM((TILE, TILE), F32),
            pltpu.VMEM((PAIR, 3 * qh.shape[0], 2 * TILE), BF16),
            pltpu.VMEM((TILE * beams, TILE), F32),
            pltpu.VMEM((TILE * beams, TILE), F32),
            pltpu.VMEM((beams // 2, 2 * TILE, TILE), F32),
            pltpu.VMEM((beams // 2, 2 * TILE, TILE), F32),
            pltpu.SemaphoreType.DMA((beams // 2,)),
            pltpu.SemaphoreType.DMA((beams // 2,)),
        ],
        compiler_params=pltpu.CompilerParams(
            collective_id=1, has_side_effects=True, vmem_limit_bytes=LIMIT
        ),
        name="beams",
    )(beam_tilts.T, crop_anchor, qh, ql, t1, dh, dl, drow, probe_spots.swapaxes(1, 2), weights)


def solution(mesh):
    placed = (P("groups", "beam", None), P(), P(), P(), P("groups", None, None), P("groups"))
    return jax.shard_map(
        functools.partial(per_device, n=mesh.shape["beam"]),
        mesh=mesh,
        in_specs=placed,
        out_specs=P(("groups", "beam"), None, None),
        check_vma=False,
    )
```
